32 devices in a mesh: dp: 4 (over y, x), mp: 8 (over z, core).
Axes of the slice: x: 2, y: 2, z: 4, core: 2. Of those that a mesh axis runs over, the one named last changes fastest.
Arguments:
- tokens_in: bfloat16 [4096, 4096], P('dp', 'mp'), may hold values from -6 to 6
- grad_out: bfloat16 [4096, 14336], P('dp', 'mp'), may hold values from -6 to 6
- old_first: float32 [128, 32, 14336], P(None, ('dp', 'mp')), may hold values from -2 to 2
- old_second: float32 [128, 32, 14336], P(None, ('dp', 'mp')), may hold values from 0.01 to 1
- old_master: float32 [128, 32, 14336], P(None, ('dp', 'mp')), may hold values from -6 to 6
- step_count: int32 [1], replicated, may hold values from 1 to 31
Outputs:
- new_first: float32 [4096, 14336], P('dp', 'mp')
- new_second: float32 [4096, 14336], P('dp', 'mp')
- new_weights: float32 [4096, 14336], P(None, 'mp')
The draws below stay inside these ranges and needn't reach their ends.
All inputs are finite; a program needn't handle non-finite values.
Results may differ from the reference program's by a relative error of at most 0.0003.
Values may be sent and summed in bfloat16 or wider, within the bound.
A program may use at most 192 MiB of HBM per device.

```python
import math
import jax
import jax.numpy as jnp
from jax import lax

D = 4096
FF = 14336
TOK_DEV = 1024
TOKENS = 4096
OLD_ROWS = 128
DEVICES = 32


def block_scale(own_key, shape, cuts, smallest, largest):
    level, own = 1.0, jax.random.fold_in(own_key, 6)
    for dim, parts in cuts:
        steps = jnp.exp(jax.random.uniform(jax.random.fold_in(own, dim), (parts,), jnp.float32, smallest / len(cuts), largest / len(cuts)))
        level = level * jnp.repeat(steps, shape[dim] // parts).reshape([-1 if axis == dim else 1 for axis in range(len(shape))])
    return level


def gaussian(stream_key, shape, spread, most, split=(), held_as=jnp.bfloat16):
    level = block_scale(stream_key, shape, split, -0.22, 0.18) if split else 1.0
    drawn = jax.random.normal(stream_key, shape, jnp.float32) * spread * level
    return jnp.minimum(jnp.maximum(drawn, -most), most).astype(held_as)


def setup_inputs(seed: int = 0) -> dict:
    splits = jax.random.split(jax.random.key(seed), 7)
    return {
        "tokens_in": gaussian(splits[0], (TOKENS, D), 1.0, 6.0, ((0, 4), (1, 8))),
        "grad_out": gaussian(splits[1], (TOKENS, FF), 1.0, 6.0, ((0, 4), (1, 8))),
        "old_first": gaussian(splits[2], (OLD_ROWS, DEVICES, FF), 0.3, 2.0, ((1, 32),), jnp.float32),
        "old_second": jnp.clip(jnp.exp(math.log(1.0) - 4.6051702 * jax.random.uniform(splits[3], (OLD_ROWS, DEVICES, FF), jnp.float32) ** block_scale(splits[3], (OLD_ROWS, DEVICES, FF), ((1, 32),), -0.2, 0.2)), 0.01, 1.0),
        "old_master": gaussian(splits[4], (OLD_ROWS, DEVICES, FF), 1.0, 6.0, ((1, 32),), jnp.float32),
        "step_count": jax.random.randint(splits[5], (1,), 1, 32).astype(jnp.int32),
    }


def reference(tokens_in, grad_out, old_first, old_second, old_master, step_count):
    first = old_first.reshape(D, FF)
    second = old_second.reshape(D, FF)
    master = old_master.reshape(D, FF)
    grad_scale = 1.0 / jnp.sqrt(jnp.float32(TOKENS))
    group_count = TOKENS // TOK_DEV

    def add_group(total, group):
        start = (group * TOK_DEV).astype(jnp.int32)
        rows_in = lax.dynamic_slice_in_dim(tokens_in, start, TOK_DEV, 0)
        rows_out = lax.dynamic_slice_in_dim(grad_out, start, TOK_DEV, 0)
        partial_value = jnp.dot(rows_in.T, rows_out, preferred_element_type=jnp.float32) * grad_scale
        return (total + partial_value, None)
    grad, _ = lax.scan(add_group, jnp.zeros((D, FF), jnp.float32), jnp.arange(group_count, dtype=jnp.int32))
    new_first = 0.9 * first + 0.1 * grad
    new_second = 0.95 * second + 0.05 * grad * grad
    step_float = step_count[0].astype(jnp.float32)
    correct_one = 1.0 - jnp.power(jnp.float32(0.9), step_float)
    correct_two = 1.0 - jnp.power(jnp.float32(0.95), step_float)
    update = new_first / correct_one / (jnp.sqrt(new_second / correct_two) + 1e-08)
    new_weights = master - 0.02 * (update + 0.1 * master)
    return (new_first, new_second, new_weights)
```

```python
import functools
import math

import jax
import jax.numpy as jnp
from jax import lax
from jax.experimental import pallas as pl
from jax.experimental.pallas import tpu as pltpu
from jax.sharding import PartitionSpec as P

LANES = 128
HALVES = 2
TOP_CODE = 32767.0
VMEM_LIMIT = 56 * 1024 * 1024


def plain(tokens_in, grad_out, old_first, old_second, old_master, step_count):
    dp_count = lax.axis_size("dp")
    mp_count = lax.axis_size("mp")
    device_total = dp_count * mp_count
    tok_rows = tokens_in.shape[0]
    col_width = grad_out.shape[1]
    grad_scale = 1.0 / math.sqrt(tok_rows * dp_count)
    contract = (((0,), (0,)), ((), ()))
    product = lax.dot_general(
        lax.all_gather(tokens_in, "mp", axis=1, tiled=True),
        grad_out,
        contract,
        preferred_element_type=jnp.float32,
    )
    partial_value = product * grad_scale
    grad = lax.psum_scatter(partial_value, "dp", scatter_dimension=0, tiled=True)
    run_rows = old_first.shape[0] // dp_count

    def arrange(state):
        blocks = state.reshape(dp_count, run_rows, mp_count, col_width)
        return blocks.transpose(1, 0, 2, 3).reshape(run_rows, device_total, col_width)

    moved = (
        lax.all_to_all(arrange(old_first), ("dp", "mp"), split_axis=1, concat_axis=1, tiled=True),
        lax.all_to_all(arrange(old_second), ("dp", "mp"), split_axis=1, concat_axis=1, tiled=True),
        lax.all_to_all(arrange(old_master), ("dp", "mp"), split_axis=1, concat_axis=1, tiled=True),
    )
    first, second, master = [item.reshape(run_rows * device_total, col_width) for item in moved]
    new_first = 0.9 * first + 0.1 * grad
    new_second = 0.95 * second + 0.05 * grad * grad
    step_float = step_count[0].astype(jnp.float32)
    correct_one = 1.0 - jnp.power(jnp.float32(0.9), step_float)
    correct_two = 1.0 - jnp.power(jnp.float32(0.95), step_float)
    update = new_first / correct_one / (jnp.sqrt(new_second / correct_two) + 1e-08)
    new_master = master - 0.02 * (update + 0.1 * master)
    new_weights = lax.all_gather(new_master, "dp", axis=0, tiled=True)
    return (new_first, new_second, new_weights)


def coded(value):
    top = jnp.maximum(jnp.max(jnp.abs(value), axis=1, keepdims=True), 1e-30)
    return jnp.round(value * (TOP_CODE / top)).astype(jnp.int16), top


def encode_kernel(rows, groups, first_ref, second_ref, master_ref, code_ref, top_ref):
    blocks = code_ref.shape[0]
    per_row = blocks * groups
    lane = lax.broadcasted_iota(jnp.int32, (rows, LANES), 1)

    def block(index, carry):
        tops = jnp.zeros((rows, LANES), jnp.float32)
        for which, ref in enumerate((first_ref, second_ref, master_ref)):
            for group in range(groups):
                value = ref[0, 0, pl.ds(index * groups + group, rows, stride=per_row), :]
                code, top = coded(value)
                code_ref[index, which * rows : (which + 1) * rows, group * LANES : (group + 1) * LANES] = code
                tops = jnp.where(lane == which * groups + group, top, tops)
        top_ref[index] = tops
        return carry

    lax.fori_loop(0, blocks, block, 0)


def encode(half, states, dp_count, mp_count, col_width):
    run_rows = states[0].shape[0] // dp_count
    rows = run_rows // HALVES
    groups = col_width // LANES
    flat = [item.reshape(dp_count, HALVES, rows * mp_count * groups, LANES) for item in states]
    spec = pl.BlockSpec((1, 1, rows * mp_count * groups, LANES), lambda d: (d, half, 0, 0))
    return pl.pallas_call(
        functools.partial(encode_kernel, rows, groups),
        grid=(dp_count,),
        in_specs=[spec] * 3,
        out_specs=(
            pl.BlockSpec((mp_count, 3 * rows, col_width), lambda d: (d, 0, 0)),
            pl.BlockSpec((mp_count, rows, LANES), lambda d: (d, 0, 0)),
        ),
        out_shape=(
            jax.ShapeDtypeStruct((dp_count * mp_count, 3 * rows, col_width), jnp.int16),
            jax.ShapeDtypeStruct((dp_count * mp_count, rows, LANES), jnp.float32),
        ),
        compiler_params=pltpu.CompilerParams(vmem_limit_bytes=VMEM_LIMIT),
    )(*flat)


def adam_kernel(rows, devices, groups, code_ref, top_ref, grad_ref, scale_ref, *rest):
    first_ref, second_ref, code_out, top_out, held = rest[-5:]
    group = pl.program_id(0)
    correct_one = scale_ref[0]
    correct_two = scale_ref[1]
    lane = lax.broadcasted_iota(jnp.int32, (devices * rows, LANES), 1)
    tops = top_ref[...].reshape(devices * rows, LANES)
    for which in range(3):
        code = code_ref[:, which * rows : (which + 1) * rows, :].astype(jnp.float32)
        picked = jnp.where(lane == which * groups + group, tops, 0.0)
        top = jnp.sum(picked, axis=1, keepdims=True)
        held[which] = code.reshape(devices * rows, LANES) * (top * (1.0 / TOP_CODE))
    out_lane = lax.broadcasted_iota(jnp.int32, (devices, LANES), 1)

    @pl.when(group == 0)
    def _():
        top_out[...] = jnp.zeros_like(top_out)

    def step(row, carry):
        first = held[0, pl.ds(row, devices, stride=rows), :]
        second = held[1, pl.ds(row, devices, stride=rows), :]
        master = held[2, pl.ds(row, devices, stride=rows), :]
        place = pl.ds(pl.multiple_of(row * devices, devices), devices)
        grad = grad_ref[place, :]
        new_first = 0.9 * first + 0.1 * grad
        new_second = 0.95 * second + 0.05 * grad * grad
        update = new_first / correct_one / (jnp.sqrt(new_second / correct_two) + 1e-08)
        weights = master - 0.02 * (update + 0.1 * master)
        code, top = coded(weights)
        first_ref[place, :] = new_first
        second_ref[place, :] = new_second
        code_out[place, :] = code
        top_out[place, :] = jnp.where(out_lane == group, top, top_out[place, :])
        return carry

    lax.fori_loop(0, rows, step, 0)


def adam(half, codes, tops, grad, corrections, previous):
    devices, rows = tops.shape[:2]
    col_width = codes.shape[2]
    groups = col_width // LANES
    height = devices * rows
    block = pl.BlockSpec((height, LANES), lambda c: (half, c))
    return pl.pallas_call(
        functools.partial(adam_kernel, rows, devices, groups),
        grid=(groups,),
        in_specs=[
            pl.BlockSpec((devices, 3 * rows, LANES), lambda c: (0, 0, c)),
            pl.BlockSpec((devices, rows, LANES), lambda c: (0, 0, 0)),
            block,
            pl.BlockSpec(memory_space=pltpu.SMEM),
        ]
        + [pl.BlockSpec(memory_space=pl.ANY)] * len(previous),
        out_specs=(
            block,
            block,
            pl.BlockSpec((height, LANES), lambda c: (0, c)),
            pl.BlockSpec((height, LANES), lambda c: (0, 0)),
        ),
        out_shape=(
            jax.ShapeDtypeStruct(grad.shape, jnp.float32),
            jax.ShapeDtypeStruct(grad.shape, jnp.float32),
            jax.ShapeDtypeStruct((height, col_width), jnp.int16),
            jax.ShapeDtypeStruct((height, LANES), jnp.float32),
        ),
        scratch_shapes=[pltpu.VMEM((3, height, LANES), jnp.float32)],
        input_output_aliases={4: 0, 5: 1} if previous else {},
        compiler_params=pltpu.CompilerParams(vmem_limit_bytes=VMEM_LIMIT),
    )(codes, tops, grad, corrections, *previous)


def decode_kernel(groups, code_ref, top_ref, *rest):
    out_ref = rest[-1]
    for group in range(groups):
        columns = slice(group * LANES, (group + 1) * LANES)
        scale = top_ref[0, :, group : group + 1] * (1.0 / TOP_CODE)
        out_ref[0, :, columns] = code_ref[0, :, columns].astype(jnp.float32) * scale


def decode(half, codes, tops, previous):
    dp_count, height, col_width = codes.shape
    groups = col_width // LANES
    tile = height // 2
    return pl.pallas_call(
        functools.partial(decode_kernel, groups),
        grid=(dp_count, 2),
        in_specs=[
            pl.BlockSpec((1, tile, col_width), lambda d, t: (d, t, 0)),
            pl.BlockSpec((1, tile, tops.shape[2]), lambda d, t: (d, t, 0)),
        ]
        + [pl.BlockSpec(memory_space=pl.ANY)] * len(previous),
        out_specs=pl.BlockSpec((1, tile, col_width), lambda d, t: (d, 2 * half + t, 0)),
        out_shape=jax.ShapeDtypeStruct((dp_count, HALVES * height, col_width), jnp.float32),
        input_output_aliases={2: 0} if previous else {},
        compiler_params=pltpu.CompilerParams(vmem_limit_bytes=VMEM_LIMIT),
    )(codes, tops, *previous)


def local(tokens_in, grad_out, old_first, old_second, old_master, step_count):
    dp_count = lax.axis_size("dp")
    mp_count = lax.axis_size("mp")
    device_total = dp_count * mp_count
    tok_rows = tokens_in.shape[0]
    col_width = grad_out.shape[1]
    run_rows = old_first.shape[0] // dp_count
    groups = col_width // LANES
    if run_rows % (16 * HALVES) or col_width % LANES or 3 * groups > LANES or device_total % 32:
        return plain(tokens_in, grad_out, old_first, old_second, old_master, step_count)
    both = ("dp", "mp")
    states = (old_first, old_second, old_master)
    moved = []
    for half in range(HALVES):
        codes, tops = encode(half, states, dp_count, mp_count, col_width)
        moved.append(
            [lax.all_to_all(item, both, split_axis=0, concat_axis=0, tiled=True) for item in (tops, codes)]
        )
    grad_scale = 1.0 / math.sqrt(tok_rows * dp_count)
    all_out = lax.all_gather(grad_out, "dp", axis=0, tiled=True)
    features = lax.all_gather(tokens_in, "mp", axis=1, tiled=True)
    features = lax.all_to_all(features, "dp", split_axis=1, concat_axis=0, tiled=True)
    grad = (
        lax.dot_general(features, all_out, (((0,), (0,)), ((), ())), preferred_element_type=jnp.float32)
        * grad_scale
    )
    step_float = step_count[0].astype(jnp.float32)
    corrections = jnp.stack(
        [1.0 - jnp.power(jnp.float32(0.9), step_float), 1.0 - jnp.power(jnp.float32(0.95), step_float)]
    )
    previous, sent = (), []
    for half in range(HALVES):
        tops, codes = moved[half]
        new_first, new_second, code, top = adam(half, codes, tops, grad, corrections, previous)
        previous = (new_first, new_second)
        height = code.shape[0]
        packed = top[:, :groups].reshape(height * groups // LANES, LANES)
        sent.append(
            (
                lax.all_gather(code, "dp", axis=0, tiled=False),
                lax.all_gather(packed, "dp", axis=0, tiled=False).reshape(dp_count, height, groups),
            )
        )
    weights = ()
    for half in range(HALVES):
        weights = (decode(half, *sent[half], weights),)
    return (*previous, weights[0].reshape(-1, col_width))


def solution(mesh):
    placed = (
        P("dp", "mp"),
        P("dp", "mp"),
        P(None, ("dp", "mp"), None),
        P(None, ("dp", "mp"), None),
        P(None, ("dp", "mp"), None),
        P(),
    )
    return jax.shard_map(
        local,
        mesh=mesh,
        in_specs=placed,
        out_specs=(P("dp", "mp"), P("dp", "mp"), P(None, "mp")),
        check_vma=False,
    )
```

```python
import functools
import math

import jax
import jax.numpy as jnp
from jax import lax
from jax.experimental import pallas as pl
from jax.experimental.pallas import tpu as pltpu
from jax.sharding import PartitionSpec as P

LANES = 128
HALVES = 2
TOP_CODE = 32767.0
VMEM_LIMIT = 56 * 1024 * 1024


def plain(tokens_in, grad_out, old_first, old_second, old_master, step_count):
    dp_count = lax.axis_size("dp")
    mp_count = lax.axis_size("mp")
    device_total = dp_count * mp_count
    tok_rows = tokens_in.shape[0]
    col_width = grad_out.shape[1]
    grad_scale = 1.0 / math.sqrt(tok_rows * dp_count)
    contract = (((0,), (0,)), ((), ()))
    product = lax.dot_general(
        lax.all_gather(tokens_in, "mp", axis=1, tiled=True),
        grad_out,
        contract,
        preferred_element_type=jnp.float32,
    )
    partial_value = product * grad_scale
    grad = lax.psum_scatter(partial_value, "dp", scatter_dimension=0, tiled=True)
    run_rows = old_first.shape[0] // dp_count

    def arrange(state):
        blocks = state.reshape(dp_count, run_rows, mp_count, col_width)
        return blocks.transpose(1, 0, 2, 3).reshape(run_rows, device_total, col_width)

    moved = (
        lax.all_to_all(arrange(old_first), ("dp", "mp"), split_axis=1, concat_axis=1, tiled=True),
        lax.all_to_all(arrange(old_second), ("dp", "mp"), split_axis=1, concat_axis=1, tiled=True),
        lax.all_to_all(arrange(old_master), ("dp", "mp"), split_axis=1, concat_axis=1, tiled=True),
    )
    first, second, master = [item.reshape(run_rows * device_total, col_width) for item in moved]
    new_first = 0.9 * first + 0.1 * grad
    new_second = 0.95 * second + 0.05 * grad * grad
    step_float = step_count[0].astype(jnp.float32)
    correct_one = 1.0 - jnp.power(jnp.float32(0.9), step_float)
    correct_two = 1.0 - jnp.power(jnp.float32(0.95), step_float)
    update = new_first / correct_one / (jnp.sqrt(new_second / correct_two) + 1e-08)
    new_master = master - 0.02 * (update + 0.1 * master)
    new_weights = lax.all_gather(new_master, "dp", axis=0, tiled=True)
    return (new_first, new_second, new_weights)


def coded(value):
    top = jnp.maximum(jnp.max(jnp.abs(value), axis=1, keepdims=True), 1e-30)
    return jnp.round(value * (TOP_CODE / top)).astype(jnp.int16), top


def encode_kernel(rows, groups, first_ref, second_ref, master_ref, code_ref, top_ref):
    blocks = code_ref.shape[0]
    per_row = blocks * groups
    lane = lax.broadcasted_iota(jnp.int32, (rows, LANES), 1)

    def block(index, carry):
        tops = jnp.zeros((rows, LANES), jnp.float32)
        for which, ref in enumerate((first_ref, second_ref, master_ref)):
            for group in range(groups):
                value = ref[0, 0, pl.ds(index * groups + group, rows, stride=per_row), :]
                code, top = coded(value)
                code_ref[index, which * rows : (which + 1) * rows, group * LANES : (group + 1) * LANES] = code
                tops = jnp.where(lane == which * groups + group, top, tops)
        top_ref[index] = tops
        return carry

    lax.fori_loop(0, blocks, block, 0)


def encode(half, states, dp_count, mp_count, col_width):
    run_rows = states[0].shape[0] // dp_count
    rows = run_rows // HALVES
    groups = col_width // LANES
    flat = [item.reshape(dp_count, HALVES, rows * mp_count * groups, LANES) for item in states]
    spec = pl.BlockSpec((1, 1, rows * mp_count * groups, LANES), lambda d: (d, half, 0, 0))
    return pl.pallas_call(
        functools.partial(encode_kernel, rows, groups),
        grid=(dp_count,),
        in_specs=[spec] * 3,
        out_specs=(
            pl.BlockSpec((mp_count, 3 * rows, col_width), lambda d: (d, 0, 0)),
            pl.BlockSpec((mp_count, rows, LANES), lambda d: (d, 0, 0)),
        ),
        out_shape=(
            jax.ShapeDtypeStruct((dp_count * mp_count, 3 * rows, col_width), jnp.int16),
            jax.ShapeDtypeStruct((dp_count * mp_count, rows, LANES), jnp.float32),
        ),
        compiler_params=pltpu.CompilerParams(vmem_limit_bytes=VMEM_LIMIT),
    )(*flat)


def adam_kernel(rows, devices, groups, code_ref, top_ref, grad_ref, scale_ref, *rest):
    first_ref, second_ref, code_out, top_out, held = rest[-5:]
    group = pl.program_id(0)
    correct_one = scale_ref[0]
    correct_two = scale_ref[1]
    lane = lax.broadcasted_iota(jnp.int32, (devices * rows, LANES), 1)
    tops = top_ref[...].reshape(devices * rows, LANES)
    for which in range(3):
        code = code_ref[:, which * rows : (which + 1) * rows, :].astype(jnp.float32)
        picked = jnp.where(lane == which * groups + group, tops, 0.0)
        top = jnp.sum(picked, axis=1, keepdims=True)
        held[which] = code.reshape(devices * rows, LANES) * (top * (1.0 / TOP_CODE))
    out_lane = lax.broadcasted_iota(jnp.int32, (devices, LANES), 1)

    @pl.when(group == 0)
    def _():
        top_out[...] = jnp.zeros_like(top_out)

    def step(row, carry):
        first = held[0, pl.ds(row, devices, stride=rows), :]
        second = held[1, pl.ds(row, devices, stride=rows), :]
        master = held[2, pl.ds(row, devices, stride=rows), :]
        place = pl.ds(pl.multiple_of(row * devices, devices), devices)
        grad = grad_ref[place, :]
        new_first = 0.9 * first + 0.1 * grad
        new_second = 0.95 * second + 0.05 * grad * grad
        update = new_first / correct_one / (jnp.sqrt(new_second / correct_two) + 1e-08)
        weights = master - 0.02 * (update + 0.1 * master)
        code, top = coded(weights)
        first_ref[place, :] = new_first
        second_ref[place, :] = new_second
        code_out[place, :] = code
        top_out[place, :] = jnp.where(out_lane == group, top, top_out[place, :])
        return carry

    lax.fori_loop(0, rows, step, 0, unroll=4)


def adam(half, codes, tops, grad, corrections, previous):
    devices, rows = tops.shape[:2]
    col_width = codes.shape[2]
    groups = col_width // LANES
    height = devices * rows
    block = pl.BlockSpec((height, LANES), lambda c: (half, c))
    return pl.pallas_call(
        functools.partial(adam_kernel, rows, devices, groups),
        grid=(groups,),
        in_specs=[
            pl.BlockSpec((devices, 3 * rows, LANES), lambda c: (0, 0, c)),
            pl.BlockSpec((devices, rows, LANES), lambda c: (0, 0, 0)),
            block,
            pl.BlockSpec(memory_space=pltpu.SMEM),
        ]
        + [pl.BlockSpec(memory_space=pl.ANY)] * len(previous),
        out_specs=(
            block,
            block,
            pl.BlockSpec((height, LANES), lambda c: (0, c)),
            pl.BlockSpec((height, LANES), lambda c: (0, 0)),
        ),
        out_shape=(
            jax.ShapeDtypeStruct(grad.shape, jnp.float32),
            jax.ShapeDtypeStruct(grad.shape, jnp.float32),
            jax.ShapeDtypeStruct((height, col_width), jnp.int16),
            jax.ShapeDtypeStruct((height, LANES), jnp.float32),
        ),
        scratch_shapes=[pltpu.VMEM((3, height, LANES), jnp.float32)],
        input_output_aliases={4: 0, 5: 1} if previous else {},
        compiler_params=pltpu.CompilerParams(vmem_limit_bytes=VMEM_LIMIT),
    )(codes, tops, grad, corrections, *previous)


def decode_kernel(groups, code_ref, top_ref, *rest):
    out_ref = rest[-1]
    for group in range(groups):
        columns = slice(group * LANES, (group + 1) * LANES)
        scale = top_ref[0, :, group : group + 1] * (1.0 / TOP_CODE)
        out_ref[0, :, columns] = code_ref[0, :, columns].astype(jnp.float32) * scale


def decode(half, codes, tops, previous):
    dp_count, height, col_width = codes.shape
    groups = col_width // LANES
    tile = height // 2
    return pl.pallas_call(
        functools.partial(decode_kernel, groups),
        grid=(dp_count, 2),
        in_specs=[
            pl.BlockSpec((1, tile, col_width), lambda d, t: (d, t, 0)),
            pl.BlockSpec((1, tile, tops.shape[2]), lambda d, t: (d, t, 0)),
        ]
        + [pl.BlockSpec(memory_space=pl.ANY)] * len(previous),
        out_specs=pl.BlockSpec((1, tile, col_width), lambda d, t: (d, 2 * half + t, 0)),
        out_shape=jax.ShapeDtypeStruct((dp_count, HALVES * height, col_width), jnp.float32),
        input_output_aliases={2: 0} if previous else {},
        compiler_params=pltpu.CompilerParams(vmem_limit_bytes=VMEM_LIMIT),
    )(codes, tops, *previous)


def local(tokens_in, grad_out, old_first, old_second, old_master, step_count):
    dp_count = lax.axis_size("dp")
    mp_count = lax.axis_size("mp")
    device_total = dp_count * mp_count
    tok_rows = tokens_in.shape[0]
    col_width = grad_out.shape[1]
    run_rows = old_first.shape[0] // dp_count
    groups = col_width // LANES
    if run_rows % (16 * HALVES) or col_width % LANES or 3 * groups > LANES or device_total % 32:
        return plain(tokens_in, grad_out, old_first, old_second, old_master, step_count)
    both = ("dp", "mp")
    states = (old_first, old_second, old_master)
    grad_scale = 1.0 / math.sqrt(tok_rows * dp_count)
    features = lax.all_gather(tokens_in, "mp", axis=1, tiled=True)
    product = lax.dot_general(
        features, grad_out, (((0,), (0,)), ((), ())), preferred_element_type=jnp.float32
    )
    grad = lax.psum_scatter(product * grad_scale, "dp", scatter_dimension=0, tiled=True)
    coded_states = [encode(half, states, dp_count, mp_count, col_width) for half in range(HALVES)]
    all_tops = lax.all_to_all(
        jnp.concatenate([tops for _, tops in coded_states], axis=1),
        both,
        split_axis=0,
        concat_axis=0,
        tiled=True,
    )
    rows = run_rows // HALVES
    moved = [
        (
            all_tops[:, half * rows : (half + 1) * rows],
            lax.all_to_all(codes, both, split_axis=0, concat_axis=0, tiled=True),
        )
        for half, (codes, _) in enumerate(coded_states)
    ]
    step_float = step_count[0].astype(jnp.float32)
    corrections = jnp.stack(
        [1.0 - jnp.power(jnp.float32(0.9), step_float), 1.0 - jnp.power(jnp.float32(0.95), step_float)]
    )
    previous, sent = (), []
    for half in range(HALVES):
        tops, codes = moved[half]
        new_first, new_second, code, top = adam(half, codes, tops, grad, corrections, previous)
        previous = (new_first, new_second)
        height = code.shape[0]
        packed = top[:, :groups].reshape(height * groups // LANES, LANES)
        sent.append(
            (
                lax.all_gather(code, "dp", axis=0, tiled=False),
                lax.all_gather(packed, "dp", axis=0, tiled=False).reshape(dp_count, height, groups),
            )
        )
    weights = ()
    for half in range(HALVES):
        weights = (decode(half, *sent[half], weights),)
    return (*previous, weights[0].reshape(-1, col_width))


def solution(mesh):
    placed = (
        P("dp", "mp"),
        P("dp", "mp"),
        P(None, ("dp", "mp"), None),
        P(None, ("dp", "mp"), None),
        P(None, ("dp", "mp"), None),
        P(),
    )
    return jax.shard_map(
        local,
        mesh=mesh,
        in_specs=placed,
        out_specs=(P("dp", "mp"), P("dp", "mp"), P(None, "mp")),
        check_vma=False,
    )
```

```python
import functools
import math

import jax
import jax.numpy as jnp
from jax import lax
from jax.experimental import pallas as pl
from jax.experimental.pallas import tpu as pltpu
from jax.sharding import PartitionSpec as P

LANES = 128
HALVES = 2
TOP_CODE = 32767.0
VMEM_LIMIT = 56 * 1024 * 1024


def plain(tokens_in, grad_out, old_first, old_second, old_master, step_count):
    dp_count = lax.axis_size("dp")
    mp_count = lax.axis_size("mp")
    device_total = dp_count * mp_count
    tok_rows = tokens_in.shape[0]
    col_width = grad_out.shape[1]
    grad_scale = 1.0 / math.sqrt(tok_rows * dp_count)
    contract = (((0,), (0,)), ((), ()))
    product = lax.dot_general(
        lax.all_gather(tokens_in, "mp", axis=1, tiled=True),
        grad_out,
        contract,
        preferred_element_type=jnp.float32,
    )
    partial_value = product * grad_scale
    grad = lax.psum_scatter(partial_value, "dp", scatter_dimension=0, tiled=True)
    run_rows = old_first.shape[0] // dp_count

    def arrange(state):
        blocks = state.reshape(dp_count, run_rows, mp_count, col_width)
        return blocks.transpose(1, 0, 2, 3).reshape(run_rows, device_total, col_width)

    moved = (
        lax.all_to_all(arrange(old_first), ("dp", "mp"), split_axis=1, concat_axis=1, tiled=True),
        lax.all_to_all(arrange(old_second), ("dp", "mp"), split_axis=1, concat_axis=1, tiled=True),
        lax.all_to_all(arrange(old_master), ("dp", "mp"), split_axis=1, concat_axis=1, tiled=True),
    )
    first, second, master = [item.reshape(run_rows * device_total, col_width) for item in moved]
    new_first = 0.9 * first + 0.1 * grad
    new_second = 0.95 * second + 0.05 * grad * grad
    step_float = step_count[0].astype(jnp.float32)
    correct_one = 1.0 - jnp.power(jnp.float32(0.9), step_float)
    correct_two = 1.0 - jnp.power(jnp.float32(0.95), step_float)
    update = new_first / correct_one / (jnp.sqrt(new_second / correct_two) + 1e-08)
    new_master = master - 0.02 * (update + 0.1 * master)
    new_weights = lax.all_gather(new_master, "dp", axis=0, tiled=True)
    return (new_first, new_second, new_weights)


def coded(value):
    top = jnp.maximum(jnp.max(jnp.abs(value), axis=1, keepdims=True), 1e-30)
    return jnp.round(value * (TOP_CODE / top)).astype(jnp.int16), top


def encode_kernel(rows, groups, first_ref, second_ref, master_ref, code_ref, top_ref):
    blocks = code_ref.shape[0]
    per_row = blocks * groups
    lane = lax.broadcasted_iota(jnp.int32, (rows, LANES), 1)

    def block(index, carry):
        tops = jnp.zeros((rows, LANES), jnp.float32)
        for which, ref in enumerate((first_ref, second_ref, master_ref)):
            for group in range(groups):
                value = ref[0, 0, pl.ds(index * groups + group, rows, stride=per_row), :]
                code, top = coded(value)
                code_ref[index, which * rows : (which + 1) * rows, group * LANES : (group + 1) * LANES] = code
                tops = jnp.where(lane == which * groups + group, top, tops)
        top_ref[index] = tops
        return carry

    lax.fori_loop(0, blocks, block, 0)


def encode(half, states, dp_count, mp_count, col_width):
    run_rows = states[0].shape[0] // dp_count
    rows = run_rows // HALVES
    groups = col_width // LANES
    flat = [item.reshape(dp_count, HALVES, rows * mp_count * groups, LANES) for item in states]
    spec = pl.BlockSpec((1, 1, rows * mp_count * groups, LANES), lambda d: (d, half, 0, 0))
    return pl.pallas_call(
        functools.partial(encode_kernel, rows, groups),
        grid=(dp_count,),
        in_specs=[spec] * 3,
        out_specs=(
            pl.BlockSpec((mp_count, 3 * rows, col_width), lambda d: (d, 0, 0)),
            pl.BlockSpec((mp_count, rows, LANES), lambda d: (d, 0, 0)),
        ),
        out_shape=(
            jax.ShapeDtypeStruct((dp_count * mp_count, 3 * rows, col_width), jnp.int16),
            jax.ShapeDtypeStruct((dp_count * mp_count, rows, LANES), jnp.float32),
        ),
        compiler_params=pltpu.CompilerParams(vmem_limit_bytes=VMEM_LIMIT),
    )(*flat)


def adam_kernel(rows, devices, groups, code_ref, top_ref, grad_ref, scale_ref, *rest):
    first_ref, second_ref, code_out, top_out, held = rest[-5:]
    group = pl.program_id(0)
    correct_one = scale_ref[0]
    correct_two = scale_ref[1]
    lane = lax.broadcasted_iota(jnp.int32, (devices * rows, LANES), 1)
    tops = top_ref[...].reshape(devices * rows, LANES)
    for which in range(3):
        code = code_ref[:, which * rows : (which + 1) * rows, :].astype(jnp.float32)
        picked = jnp.where(lane == which * groups + group, tops, 0.0)
        top = jnp.sum(picked, axis=1, keepdims=True)
        held[which] = code.reshape(devices * rows, LANES) * (top * (1.0 / TOP_CODE))
    out_lane = lax.broadcasted_iota(jnp.int32, (devices, LANES), 1)

    @pl.when(group == 0)
    def _():
        top_out[...] = jnp.zeros_like(top_out)

    def step(row, carry):
        first = held[0, pl.ds(row, devices, stride=rows), :]
        second = held[1, pl.ds(row, devices, stride=rows), :]
        master = held[2, pl.ds(row, devices, stride=rows), :]
        place = pl.ds(pl.multiple_of(row * devices, devices), devices)
        grad = grad_ref[place, :]
        new_first = 0.9 * first + 0.1 * grad
        new_second = 0.95 * second + 0.05 * grad * grad
        update = new_first / correct_one / (jnp.sqrt(new_second / correct_two) + 1e-08)
        weights = master - 0.02 * (update + 0.1 * master)
        code, top = coded(weights)
        first_ref[place, :] = new_first
        second_ref[place, :] = new_second
        code_out[place, :] = code
        top_out[place, :] = jnp.where(out_lane == group, top, top_out[place, :])
        return carry

    lax.fori_loop(0, rows, step, 0, unroll=4)


def adam(half, codes, tops, grad, corrections, previous):
    devices, rows = tops.shape[:2]
    col_width = codes.shape[2]
    groups = col_width // LANES
    height = devices * rows
    block = pl.BlockSpec((height, LANES), lambda c: (half, c))
    return pl.pallas_call(
        functools.partial(adam_kernel, rows, devices, groups),
        grid=(groups,),
        in_specs=[
            pl.BlockSpec((devices, 3 * rows, LANES), lambda c: (0, 0, c)),
            pl.BlockSpec((devices, rows, LANES), lambda c: (0, 0, 0)),
            block,
            pl.BlockSpec(memory_space=pltpu.SMEM),
        ]
        + [pl.BlockSpec(memory_space=pl.ANY)] * len(previous),
        out_specs=(
            block,
            block,
            pl.BlockSpec((height, LANES), lambda c: (0, c)),
            pl.BlockSpec((height, LANES), lambda c: (0, 0)),
        ),
        out_shape=(
            jax.ShapeDtypeStruct(grad.shape, jnp.float32),
            jax.ShapeDtypeStruct(grad.shape, jnp.float32),
            jax.ShapeDtypeStruct((height, col_width), jnp.int16),
            jax.ShapeDtypeStruct((height, LANES), jnp.float32),
        ),
        scratch_shapes=[pltpu.VMEM((3, height, LANES), jnp.float32)],
        input_output_aliases={4: 0, 5: 1} if previous else {},
        compiler_params=pltpu.CompilerParams(vmem_limit_bytes=VMEM_LIMIT),
    )(codes, tops, grad, corrections, *previous)


def decode_kernel(groups, code_ref, top_ref, *rest):
    out_ref = rest[-1]
    for group in range(groups):
        columns = slice(group * LANES, (group + 1) * LANES)
        scale = top_ref[0, :, group : group + 1] * (1.0 / TOP_CODE)
        out_ref[0, :, columns] = code_ref[0, :, columns].astype(jnp.float32) * scale


def decode(half, codes, tops, previous):
    dp_count, height, col_width = codes.shape
    groups = col_width // LANES
    tile = height // 2
    return pl.pallas_call(
        functools.partial(decode_kernel, groups),
        grid=(dp_count, 2),
        in_specs=[
            pl.BlockSpec((1, tile, col_width), lambda d, t: (d, t, 0)),
            pl.BlockSpec((1, tile, tops.shape[2]), lambda d, t: (d, t, 0)),
        ]
        + [pl.BlockSpec(memory_space=pl.ANY)] * len(previous),
        out_specs=pl.BlockSpec((1, tile, col_width), lambda d, t: (d, 2 * half + t, 0)),
        out_shape=jax.ShapeDtypeStruct((dp_count, HALVES * height, col_width), jnp.float32),
        input_output_aliases={2: 0} if previous else {},
        compiler_params=pltpu.CompilerParams(vmem_limit_bytes=VMEM_LIMIT),
    )(codes, tops, *previous)


def local(tokens_in, grad_out, old_first, old_second, old_master, step_count):
    dp_count = lax.axis_size("dp")
    mp_count = lax.axis_size("mp")
    device_total = dp_count * mp_count
    tok_rows = tokens_in.shape[0]
    col_width = grad_out.shape[1]
    run_rows = old_first.shape[0] // dp_count
    groups = col_width // LANES
    if run_rows % (16 * HALVES) or col_width % LANES or 3 * groups > LANES or device_total % 32:
        return plain(tokens_in, grad_out, old_first, old_second, old_master, step_count)
    both = ("dp", "mp")
    states = (old_first, old_second, old_master)
    grad_scale = 1.0 / math.sqrt(tok_rows * dp_count)
    all_out = lax.all_gather(grad_out, "dp", axis=0, tiled=True)
    features = lax.all_gather(tokens_in, "mp", axis=1, tiled=True)
    coded_states = [encode(half, states, dp_count, mp_count, col_width) for half in range(HALVES)]
    all_tops = lax.all_to_all(
        jnp.concatenate([tops for _, tops in coded_states], axis=1),
        both,
        split_axis=0,
        concat_axis=0,
        tiled=True,
    )
    rows = run_rows // HALVES
    moved = [
        (
            all_tops[:, half * rows : (half + 1) * rows],
            lax.all_to_all(codes, both, split_axis=0, concat_axis=0, tiled=True),
        )
        for half, (codes, _) in enumerate(coded_states)
    ]
    features, moved = lax.optimization_barrier((features, moved))
    features = lax.all_to_all(features, "dp", split_axis=1, concat_axis=0, tiled=True)
    grad = grad_scale * lax.dot_general(
        features, all_out, (((0,), (0,)), ((), ())), preferred_element_type=jnp.float32
    )
    step_float = step_count[0].astype(jnp.float32)
    corrections = jnp.stack(
        [1.0 - jnp.power(jnp.float32(0.9), step_float), 1.0 - jnp.power(jnp.float32(0.95), step_float)]
    )
    previous, sent = (), []
    for half in range(HALVES):
        tops, codes = moved[half]
        new_first, new_second, code, top = adam(half, codes, tops, grad, corrections, previous)
        previous = (new_first, new_second)
        height = code.shape[0]
        packed = top[:, :groups].reshape(height * groups // LANES, LANES)
        sent.append(
            (
                lax.all_gather(code, "dp", axis=0, tiled=False),
                lax.all_gather(packed, "dp", axis=0, tiled=False).reshape(dp_count, height, groups),
            )
        )
    weights = ()
    for half in range(HALVES):
        weights = (decode(half, *sent[half], weights),)
    return (*previous, weights[0].reshape(-1, col_width))


def solution(mesh):
    placed = (
        P("dp", "mp"),
        P("dp", "mp"),
        P(None, ("dp", "mp"), None),
        P(None, ("dp", "mp"), None),
        P(None, ("dp", "mp"), None),
        P(),
    )
    return jax.shard_map(
        local,
        mesh=mesh,
        in_specs=placed,
        out_specs=(P("dp", "mp"), P("dp", "mp"), P(None, "mp")),
        check_vma=False,
    )
```
